1024 devices in a mesh: dp: 64 (over z_lo, x, core), expert: 16 (over y, z_hi).
Axes of the slice: x: 4, y: 8, z: 16 (z_hi: 2, z_lo: 8; z = z_hi * 8 + z_lo), core: 2. Of those that a mesh axis runs over, the one named last changes fastest.
Arguments:
- hidden: bfloat16 [131072, 1024], P(('dp', 'expert')), may hold values from -24 to 24
- expert_ids: int32 [131072, 1], P(('dp', 'expert')), may hold values from 0 to 15; in each aligned block of 128 rows (0 to 127, 128 to 255, ...) at most 10 rows name the same one
- gate_weights: float32 [131072, 1], P(('dp', 'expert')), may hold values from 0.2 to 1
- down_weight: bfloat16 [16, 1024, 2048], P('expert'), may hold values from -0.1875 to 0.1875
- out_grad: bfloat16 [131072, 2048], P(('dp', 'expert')), may hold values from -6 to 6
Outputs:
- layer_out: bfloat16 [131072, 2048], P(('dp', 'expert'))
- hidden_grad: bfloat16 [131072, 1024], P(('dp', 'expert'))
- gate_grad: float32 [131072, 1], P(('dp', 'expert'))
- weight_grad: float32 [16, 1024, 2048], P('expert', 'dp')
The draws below stay inside these ranges and needn't reach their ends.
Inputs may be any that keep to these rules, and one draw needn't show every extreme that they name: `expert_ids`: among the 128 rows of one device no expert is named more than 10 times, a bound that some block reaches.
All inputs are finite; a program needn't handle non-finite values.
Results may differ from the reference program's by a relative error of at most 0.0049.
Values may be sent and summed in bfloat16 or wider, within the bound.
No kernel may reach another device: no remote copies, remote signals or barrier semaphores. Data moves between devices by JAX's collectives and lax.ppermute only.
A program may use at most 64 MiB of HBM per device.

```python
import math
import jax
import jax.numpy as jnp
import numpy as np
from jax import lax

D_WIN = 2048
HID = 1024
TOK_DEV = 128
EXPERTS = 16
CAP = 10
TOKENS = 131072
N_DP = 64
N_EXPERT = 16


def raised(entries, key, source, target, shards_of, factor):
    owner, partner = [(jnp.arange(entries.shape[dim]) // (entries.shape[dim] // shards_of)).reshape([-1 if axis == dim else 1 for axis in range(entries.ndim)]) for dim in (source, target)]
    chosen = jax.random.permutation(key, shards_of)[partner]
    strong = (owner == chosen) | (owner == (partner + shards_of // 2) % shards_of)
    return jnp.where(strong, factor * entries, entries)


def level_of(key, dims, cuts, low, largest):
    loudness = 1.0
    for position, shards_of in cuts:
        draws = jax.random.uniform(jax.random.fold_in(jax.random.fold_in(key, 6), position), (shards_of,), jnp.float32, low / len(cuts), largest / len(cuts))
        loudness = loudness * jnp.repeat(jnp.exp(draws), dims[position] // shards_of).reshape((-1,) + (1,) * (len(dims) - 1 - position))
    return loudness


def shared_out(stream_key, own, number, rows, amount, top, most, skew):
    sequence = jax.random.permutation(stream_key, amount)
    heavy_load, ordinary = portions_of(amount, rows * top, most, skew, True), portions_of(amount, rows * top, most, skew, False)
    places = jnp.arange(amount)

    def named(tallies, rotation):
        used = int((tallies > 0).sum())
        fixed = max(1, used // 4)
        moved = fixed + (places - fixed + rotation * (used - fixed)) % max(1, amount - fixed)
        return jnp.zeros((amount,), jnp.int32).at[sequence[jnp.where(places < fixed, places, moved)]].set(jnp.asarray(tallies, jnp.int32))

    tallies = jnp.where(number % 4 == 0, named(heavy_load, number // 4), named(ordinary, number - number // 4 - 1))
    mixed = jax.random.permutation(jax.random.fold_in(own, 3), amount)
    giver, taker = mixed[0:amount // 2 * 2:2], mixed[1:amount // 2 * 2:2]
    slack = jnp.minimum(tallies[giver] - 1, most - tallies[taker]) // 2
    slack = jnp.where((giver == sequence[0]) | (taker == sequence[0]) | (tallies[taker] == 0), 0, jnp.maximum(slack, 0))
    moved = jax.random.randint(jax.random.fold_in(own, 4), (amount // 2,), 0, 1 << 20) % (slack + 1)
    tallies = tallies.at[giver].add(-moved).at[taker].add(moved)
    items = jnp.searchsorted(jnp.cumsum(tallies), jnp.arange(rows * top), side="right").astype(jnp.int32)
    table = items.reshape(top, rows).T
    table = table[jax.random.permutation(jax.random.fold_in(own, 1), rows)]
    rotation = jax.random.randint(jax.random.fold_in(own, 2), (rows, 1), 0, top)
    return jnp.take_along_axis(table, (jnp.arange(top)[None, :] + rotation) % top, axis=1)


def portions_of(count, total, reach, lean, full):
    loads = [(1 << 20) // math.isqrt(rank ** lean) + 1 for rank in range(1, count + 1)]
    largest = reach if full else min(reach, max(-(-total // count), total * loads[0] // sum(loads)))
    least = 1 if total - largest >= count - 1 else 0
    counts, rest = [largest] + [least] * (count - 1), total - largest - least * (count - 1)
    while rest > 0:
        free = [i for i in range(1, count) if counts[i] < largest] or [i for i in range(1, count) if counts[i] < reach]
        pool, remaining = sum([loads[i] for i in free]), rest
        for i in free:
            addition = min(reach - counts[i], max(1, remaining * loads[i] // pool), rest)
            counts[i] = counts[i] + addition
            rest = rest - addition
    return np.array(counts)


def noise(rng, dims, width, bound, shards=(), held_as=jnp.bfloat16):
    entries = width * jax.random.normal(rng, dims, jnp.float32)
    if shards:
        entries = entries * level_of(rng, dims, shards, -0.22, 0.18)
    return jnp.clip(entries, -bound, bound).astype(held_as)


def noise_with(own_key, shape, width, limit, cuts, heavy, kind=jnp.bfloat16):
    drawn = width * jax.random.normal(own_key, shape, jnp.float32)
    if cuts:
        drawn = drawn * level_of(own_key, shape, cuts, -0.22, 0.18)
    return jnp.clip(raised(drawn, jax.random.fold_in(own_key, 3), *heavy), -limit, limit).astype(kind)


def setup_inputs(seed: int = 0) -> dict:
    keys = jax.random.split(jax.random.key(seed), 6)
    hidden = noise_with(keys[0], (TOKENS, HID), 1.0, 24.0, ((0, 1024),), (0, 1, 1024, 6.0))
    expert_ids_keys = jax.random.split(jax.random.fold_in(keys[1], 1), TOKENS // TOK_DEV)
    expert_ids_turns = jax.random.permutation(jax.random.fold_in(keys[1], 3), TOKENS // TOK_DEV)
    expert_ids = jax.vmap(lambda own, number: shared_out(jax.random.fold_in(keys[1], 2), own, number, TOK_DEV, EXPERTS, 1, CAP, 1))(expert_ids_keys, expert_ids_turns).reshape((TOKENS, 1))
    gate_weights = jnp.clip(jnp.exp(math.log(1.0) - 1.609438 * jax.random.uniform(keys[2], (TOKENS, 1), jnp.float32) ** level_of(keys[2], (TOKENS, 1), ((0, 1024),), -0.2, 0.2)), 0.2, 1.0)
    down_weight = noise(keys[3], (EXPERTS, HID, D_WIN), HID ** -0.5, 0.1875, ((0, 16),))
    out_grad = noise(keys[4], (TOKENS, D_WIN), 1.0, 6.0, ((0, 1024),))
    return dict(hidden=hidden, expert_ids=expert_ids, gate_weights=gate_weights, down_weight=down_weight, out_grad=out_grad)


def reference(hidden, expert_ids, gate_weights, down_weight, out_grad):
    device_count = N_DP * N_EXPERT
    per_expert = device_count * CAP
    expert_list = expert_ids[:, 0].astype(jnp.int32)
    onehot = (expert_list.reshape(device_count, TOK_DEV)[:, :, None] == jnp.arange(EXPERTS, dtype=jnp.int32)).astype(jnp.int32)
    row_rank = jnp.sum(onehot * (jnp.cumsum(onehot, axis=1) - 1), axis=2).reshape(-1)
    device_of = jnp.arange(TOKENS, dtype=jnp.int32) // TOK_DEV
    slot_index = (expert_list * per_expert + device_of * CAP + row_rank).astype(jnp.int32)
    slot_table = jnp.full((EXPERTS * per_expert,), TOKENS, jnp.int32).at[slot_index].set(jnp.arange(TOKENS, dtype=jnp.int32))
    slot_table = slot_table.reshape(EXPERTS, per_expert)
    grad_rows = (gate_weights * out_grad.astype(jnp.float32)).astype(jnp.bfloat16)
    hidden_pad = jnp.concatenate([hidden, jnp.zeros((1, HID), hidden.dtype)], axis=0)
    grad_pad = jnp.concatenate([grad_rows, jnp.zeros((1, D_WIN), grad_rows.dtype)], axis=0)

    def one_expert(expert):
        token_rows = slot_table[expert]
        hid_rows = hidden_pad[token_rows]
        grad_part = grad_pad[token_rows]
        weight = down_weight[expert]
        projected = jnp.dot(hid_rows, weight, preferred_element_type=jnp.float32).astype(jnp.bfloat16)
        back_rows = lax.dot_general(grad_part, weight, (((1,), (1,)), ((), ())), preferred_element_type=jnp.float32).astype(jnp.bfloat16)
        weight_part = lax.dot_general(hid_rows, grad_part, (((0,), (0,)), ((), ())), preferred_element_type=jnp.float32)
        return projected, back_rows, weight_part

    proj_all, back_all, weight_grad = lax.map(one_expert, jnp.arange(EXPERTS, dtype=jnp.int32))
    projected = proj_all.reshape(-1, D_WIN)[slot_index].astype(jnp.float32)
    hidden_grad = back_all.reshape(-1, HID)[slot_index]
    layer_out = (gate_weights * projected).astype(jnp.bfloat16)
    gate_grad = jnp.sum(out_grad.astype(jnp.float32) * projected, axis=1, keepdims=True)
    return layer_out, hidden_grad, gate_grad, weight_grad
```

```python
import jax
import jax.numpy as jnp
from jax import lax
from jax.sharding import Mesh, PartitionSpec as P

F32, BF16 = jnp.float32, jnp.bfloat16
DP = ("zl", "x", "c")
NEAR = ("x", "c")
EXP = ("y", "zh")


def exchange(rows, count, axes):
    tall, wide = rows.shape
    moved = lax.all_to_all(
        rows.reshape(count, tall // count, wide), axes, split_axis=0, concat_axis=0, tiled=True
    )
    return moved.reshape(tall, wide)


def dot(a, b, dims, out=BF16):
    return lax.dot_general(a, b, (dims, ((), ())), preferred_element_type=F32).astype(out)


def shards(hidden, expert_ids, gate_weights, down_weight, out_grad):
    tok_rows, hid_width = hidden.shape
    experts = lax.axis_size(EXP)
    near, lines = lax.axis_size(NEAR), lax.axis_size("zl")
    strip = hid_width // (near * lines)
    capacity = 5 * tok_rows // (4 * experts)
    weight = down_weight[0]

    expert_list = expert_ids[:, 0]
    onehot = (expert_list[:, None] == jnp.arange(experts, dtype=jnp.int32)[None, :]).astype(
        jnp.int32
    )
    row_rank = jnp.sum(onehot * (jnp.cumsum(onehot, axis=0) - 1), axis=1)
    slot_index = expert_list * capacity + row_rank
    placer = (
        jnp.arange(experts * capacity, dtype=jnp.int32)[:, None] == slot_index[None, :]
    ).astype(BF16)

    grad_rows = (gate_weights * out_grad.astype(F32)).astype(BF16)
    grad_flat = exchange(dot(placer, grad_rows, ((1,), (0,))), experts, EXP)
    hid_rows = exchange(dot(placer, hidden, ((1,), (0,))), experts, EXP)

    grad_near = lax.all_gather(grad_flat, NEAR, axis=0, tiled=True)
    place = jnp.arange(hid_width, dtype=jnp.int32)
    owner = place // strip
    target = ((owner % near) * lines + owner // near) * strip + place % strip
    sorter = (target[:, None] == place[None, :]).astype(BF16)
    sorted_rows = dot(hid_rows, sorter, ((1,), (0,)))
    hid_near = exchange(
        sorted_rows.reshape(-1, near, lines * strip).swapaxes(0, 1).reshape(-1, lines * strip),
        near,
        NEAR,
    )
    partial_grad = dot(hid_near, grad_near, ((0,), (0,)), F32)
    weight_grad = lax.psum_scatter(partial_grad, "zl", scatter_dimension=0, tiled=True)

    proj_slots = exchange(dot(hid_rows, weight, ((1,), (0,))), experts, EXP)
    back_slots = exchange(dot(grad_flat, weight, ((1,), (1,))), experts, EXP)
    projected = dot(placer, proj_slots, ((0,), (0,)), F32)
    layer_out = (gate_weights * projected).astype(BF16)
    gate_grad = jnp.sum(out_grad.astype(F32) * projected, axis=1, keepdims=True)
    hidden_grad = dot(placer, back_slots, ((0,), (0,)))
    return (layer_out, hidden_grad, gate_grad, weight_grad[None])


def solution(mesh):
    fine = Mesh(mesh.devices.reshape(8, 4, 2, 8, 2), DP + EXP)
    tokens = P(DP + EXP, None)
    return jax.shard_map(
        shards,
        mesh=fine,
        in_specs=(tokens, tokens, tokens, P(EXP, None, None), tokens),
        out_specs=(tokens, tokens, tokens, P(EXP, DP, None)),
        check_vma=False,
    )
```

```python
import jax
import jax.numpy as jnp
from jax import lax
from jax.sharding import Mesh, PartitionSpec as P

F32, BF16, I32 = jnp.float32, jnp.bfloat16, jnp.int32
LINE = ("zq", "zp")
DP = LINE + ("x", "c")
EXP = ("y", "zh")
NEAR = ("x", "c")
SHARE = ("zp", "x", "c")
RING = ("zh",) + LINE


def exchange(blocks, axes):
    return lax.all_to_all(blocks, axes, split_axis=0, concat_axis=0, tiled=True)


def dot(a, b, dims, out=BF16):
    return lax.dot_general(a, b, (dims, ((), ())), preferred_element_type=F32).astype(out)


def chooser(wanted, count):
    return (wanted[:, None] == jnp.arange(count, dtype=I32)[None, :]).astype(BF16)


def shards(hidden, expert_ids, gate_weights, down_weight, out_grad):
    tok_rows, hid_width = hidden.shape
    out_width = out_grad.shape[1]
    columns, halves = lax.axis_size("y"), lax.axis_size("zh")
    experts = columns * halves
    xs, cs, near, lines = (lax.axis_size(axes) for axes in ("x", "c", NEAR, LINE))
    capacity = 5 * tok_rows // (4 * experts)
    slots = capacity + -capacity % 4
    block = halves * slots
    tall = columns * block
    strip = hid_width // lax.axis_size(DP)
    half = lax.axis_index("zh")
    weight = down_weight[0]

    part = hid_width // lax.axis_size(SHARE)
    share = lax.dynamic_slice_in_dim(weight, lax.axis_index(SHARE) * part, part, axis=0)
    share = lax.ppermute(share, "zh", [(0, 1), (1, 0)])

    expert_list = expert_ids[:, 0]
    onehot = (expert_list[:, None] == jnp.arange(experts, dtype=I32)[None, :]).astype(I32)
    row_rank = jnp.sum(onehot * (jnp.cumsum(onehot, axis=0) - 1), axis=1)
    slot_index = expert_list * slots + row_rank
    placer = (jnp.arange(tall, dtype=I32)[:, None] == slot_index[None, :]).astype(BF16)
    grad_rows = (gate_weights * out_grad.astype(F32)).astype(BF16)
    outgoing = jnp.concatenate(
        [dot(placer, grad_rows, ((1,), (0,))), dot(placer, hidden, ((1,), (0,)))], axis=1
    )
    arrived = exchange(outgoing.reshape(columns, block, -1), "y").reshape(tall, -1)
    arrived, share = lax.optimization_barrier((arrived, share))
    other_weight = lax.all_gather(share, SHARE, axis=0, tiled=True)
    grad_flat, hid_flat = arrived[:, :out_width], arrived[:, out_width:]

    full = jnp.arange(columns * halves * capacity, dtype=I32)
    compact = chooser(full // capacity * slots + full % capacity, tall)
    place = jnp.arange(hid_width, dtype=I32)
    in_quarter = place % (hid_width // xs)
    source = (
        in_quarter // (cs * strip) * (near * strip)
        + place // (hid_width // xs) * (cs * strip)
        + in_quarter % (cs * strip)
    )
    sorter = chooser(source, hid_width)
    hid_sorted = dot(dot(compact, hid_flat, ((1,), (0,))), sorter, ((1,), (1,)))
    grad_sorted = dot(compact, grad_flat, ((1,), (0,)))
    rows = full.shape[0]
    blocks = [
        jnp.concatenate(
            [
                hid_sorted[:, x * (hid_width // xs) : (x + 1) * (hid_width // xs)],
                grad_sorted[:, c * (out_width // cs) : (c + 1) * (out_width // cs)],
            ],
            axis=1,
        )
        for x in range(xs)
        for c in range(cs)
    ]
    near_rows = exchange(jnp.stack(blocks), NEAR).reshape(near * rows, -1)
    hid_near, grad_near = near_rows[:, : hid_width // xs], near_rows[:, hid_width // xs :]
    of_half = (jnp.arange(near * rows, dtype=I32) // capacity % halves)[:, None]
    zero = jnp.zeros((), BF16)
    by_half = jnp.concatenate(
        [jnp.where(of_half == h, hid_near, zero) for h in range(halves)], axis=1
    )
    partial_grad = dot(by_half, grad_near, ((0,), (0,)), F32)
    ring_sum = lax.psum_scatter(partial_grad, RING, scatter_dimension=0, tiled=True)

    own = (jnp.arange(tall, dtype=I32) // slots % halves)[:, None] == half
    proj = jnp.where(
        own, dot(hid_flat, weight, ((1,), (0,))), dot(hid_flat, other_weight, ((1,), (0,)))
    )
    back = jnp.where(
        own, dot(grad_flat, weight, ((1,), (1,))), dot(grad_flat, other_weight, ((1,), (1,)))
    )
    returned = exchange(
        jnp.concatenate([proj, back], axis=1).reshape(columns, block, -1), "y"
    ).reshape(tall, -1)
    returned, ring_sum = lax.optimization_barrier((returned, ring_sum))
    projected = dot(placer, returned[:, :out_width], ((0,), (0,)), F32)
    layer_out = (gate_weights * projected).astype(BF16)
    gate_grad = jnp.sum(out_grad.astype(F32) * projected, axis=1, keepdims=True)
    hidden_grad = dot(placer, returned[:, out_width:], ((0,), (0,)))

    core = lax.axis_index("c")
    kept = lax.dynamic_slice_in_dim(ring_sum, core * strip, strip, axis=0)
    given = lax.dynamic_slice_in_dim(ring_sum, (1 - core) * strip, strip, axis=0)
    taken = lax.ppermute(given, "c", [(0, 1), (1, 0)])
    first = core == 0
    weight_grad = jnp.concatenate(
        [jnp.where(first, kept, taken), jnp.where(first, taken, kept)], axis=1
    )
    return (layer_out, hidden_grad, gate_grad, weight_grad[None])


def solution(mesh):
    fine = Mesh(mesh.devices.reshape(4, 2, 4, 2, 8, 2), DP + EXP)
    tokens = P(DP + EXP, None)
    return jax.shard_map(
        shards,
        mesh=fine,
        in_specs=(tokens, tokens, tokens, P(EXP, None, None), tokens),
        out_specs=(tokens, tokens, tokens, P(EXP, DP, None)),
        check_vma=False,
    )
```

```python
import jax
import jax.numpy as jnp
from jax import lax
from jax.sharding import Mesh, PartitionSpec as P

F32, BF16, I32 = jnp.float32, jnp.bfloat16, jnp.int32
LINE = ("zq", "zp")
DP = LINE + ("x", "c")
EXP = ("y", "zh")
NEAR = ("x", "c")
SHARE = ("zp", "x", "c")
RING = ("zh",) + LINE


def exchange(blocks, axes):
    return lax.all_to_all(blocks, axes, split_axis=0, concat_axis=0, tiled=True)


def dot(a, b, dims, out=BF16):
    return lax.dot_general(a, b, (dims, ((), ())), preferred_element_type=F32).astype(out)


def chooser(wanted, count):
    return (wanted[:, None] == jnp.arange(count, dtype=I32)[None, :]).astype(BF16)


def shards(hidden, expert_ids, gate_weights, down_weight, out_grad):
    tok_rows, hid_width = hidden.shape
    out_width = out_grad.shape[1]
    columns, halves = lax.axis_size("y"), lax.axis_size("zh")
    experts = columns * halves
    xs, cs, near, lines = (lax.axis_size(axes) for axes in ("x", "c", NEAR, LINE))
    capacity = 5 * tok_rows // (4 * experts)
    slots = capacity + -capacity % 4
    block = halves * slots
    tall = columns * block
    strip = hid_width // lax.axis_size(DP)
    half = lax.axis_index("zh")
    weight = down_weight[0]

    part = hid_width // lax.axis_size(SHARE)
    share = lax.dynamic_slice_in_dim(weight, lax.axis_index(SHARE) * part, part, axis=0)
    share = lax.ppermute(share, "zh", [(0, 1), (1, 0)])

    expert_list = expert_ids[:, 0]
    onehot = (expert_list[:, None] == jnp.arange(experts, dtype=I32)[None, :]).astype(I32)
    row_rank = jnp.sum(onehot * (jnp.cumsum(onehot, axis=0) - 1), axis=1)
    slot_index = expert_list * slots + row_rank
    placer = (jnp.arange(tall, dtype=I32)[:, None] == slot_index[None, :]).astype(BF16)
    grad_rows = (gate_weights * out_grad.astype(F32)).astype(BF16)
    outgoing = jnp.concatenate(
        [dot(placer, grad_rows, ((1,), (0,))), dot(placer, hidden, ((1,), (0,)))], axis=1
    )
    arrived = exchange(outgoing.reshape(columns, block, -1), "y").reshape(tall, -1)
    arrived, share = lax.optimization_barrier((arrived, share))
    beside = lax.ppermute(share, "zp", [(0, 1), (1, 0)])
    grad_flat, hid_flat = arrived[:, :out_width], arrived[:, out_width:]

    full = jnp.arange(columns * halves * capacity, dtype=I32)
    compact = chooser(full // capacity * slots + full % capacity, tall)
    place = jnp.arange(hid_width, dtype=I32)
    in_quarter = place % (hid_width // xs)
    source = (
        in_quarter // (cs * strip) * (near * strip)
        + place // (hid_width // xs) * (cs * strip)
        + in_quarter % (cs * strip)
    )
    sorter = chooser(source, hid_width)
    hid_sorted = dot(dot(compact, hid_flat, ((1,), (0,))), sorter, ((1,), (1,)))
    grad_sorted = dot(compact, grad_flat, ((1,), (0,)))
    rows = full.shape[0]
    blocks = [
        jnp.concatenate(
            [
                hid_sorted[:, x * (hid_width // xs) : (x + 1) * (hid_width // xs)],
                grad_sorted[:, c * (out_width // cs) : (c + 1) * (out_width // cs)],
            ],
            axis=1,
        )
        for x in range(xs)
        for c in range(cs)
    ]
    near_rows = exchange(jnp.stack(blocks), NEAR).reshape(near * rows, -1)
    near_rows, share, beside = lax.optimization_barrier((near_rows, share, beside))
    even = lax.axis_index("zp") == 0
    pair = jnp.stack([jnp.where(even, share, beside), jnp.where(even, beside, share)])
    other_weight = lax.all_gather(pair, NEAR, axis=1, tiled=True).reshape(hid_width, -1)
    hid_near, grad_near = near_rows[:, : hid_width // xs], near_rows[:, hid_width // xs :]
    of_half = (jnp.arange(near * rows, dtype=I32) // capacity % halves)[:, None]
    zero = jnp.zeros((), BF16)
    by_half = jnp.concatenate(
        [jnp.where(of_half == h, hid_near, zero) for h in range(halves)], axis=1
    )
    partial_grad = dot(by_half, grad_near, ((0,), (0,)), F32)
    ring_sum = lax.psum_scatter(partial_grad, RING, scatter_dimension=0, tiled=True)

    own = (jnp.arange(tall, dtype=I32) // slots % halves)[:, None] == half
    proj = jnp.where(
        own, dot(hid_flat, weight, ((1,), (0,))), dot(hid_flat, other_weight, ((1,), (0,)))
    )
    back = jnp.where(
        own, dot(grad_flat, weight, ((1,), (1,))), dot(grad_flat, other_weight, ((1,), (1,)))
    )
    returned = exchange(
        jnp.concatenate([proj, back], axis=1).reshape(columns, block, -1), "y"
    ).reshape(tall, -1)
    returned, ring_sum = lax.optimization_barrier((returned, ring_sum))
    projected = dot(placer, returned[:, :out_width], ((0,), (0,)), F32)
    layer_out = (gate_weights * projected).astype(BF16)
    gate_grad = jnp.sum(out_grad.astype(F32) * projected, axis=1, keepdims=True)
    hidden_grad = dot(placer, returned[:, out_width:], ((0,), (0,)))

    core = lax.axis_index("c")
    kept = lax.dynamic_slice_in_dim(ring_sum, core * strip, strip, axis=0)
    given = lax.dynamic_slice_in_dim(ring_sum, (1 - core) * strip, strip, axis=0)
    taken = lax.ppermute(given, "c", [(0, 1), (1, 0)])
    first = core == 0
    weight_grad = jnp.concatenate(
        [jnp.where(first, kept, taken), jnp.where(first, taken, kept)], axis=1
    )
    return (layer_out, hidden_grad, gate_grad, weight_grad[None])


def solution(mesh):
    fine = Mesh(mesh.devices.reshape(4, 2, 4, 2, 8, 2), DP + EXP)
    tokens = P(DP + EXP, None)
    return jax.shard_map(
        shards,
        mesh=fine,
        in_specs=(tokens, tokens, tokens, P(EXP, None, None), tokens),
        out_specs=(tokens, tokens, tokens, P(EXP, DP, None)),
        check_vma=False,
    )
```

```python
import jax
import jax.numpy as jnp
from jax import lax
from jax.sharding import Mesh, PartitionSpec as P

F32, BF16, I32 = jnp.float32, jnp.bfloat16, jnp.int32
LINE = ("zq", "zp")
DP = LINE + ("x", "c")
EXP = ("y", "zh")
NEAR = ("x", "c")
SHARE = LINE + ("c",)
RING = ("zh",) + LINE + ("c",)


def exchange(blocks, axes):
    return lax.all_to_all(blocks, axes, split_axis=0, concat_axis=0, tiled=True)


def dot(a, b, dims, out=BF16):
    return lax.dot_general(a, b, (dims, ((), ())), preferred_element_type=F32).astype(out)


def chooser(wanted, count):
    return (wanted[:, None] == jnp.arange(count, dtype=I32)[None, :]).astype(BF16)


def shards(hidden, expert_ids, gate_weights, down_weight, out_grad):
    tok_rows, hid_width = hidden.shape
    out_width = out_grad.shape[1]
    columns, halves = lax.axis_size("y"), lax.axis_size("zh")
    experts = columns * halves
    xs, cs, near, lines = (lax.axis_size(axes) for axes in ("x", "c", NEAR, LINE))
    capacity = 5 * tok_rows // (4 * experts)
    slots = capacity + -capacity % 4
    block = halves * slots
    tall = columns * block
    strip = hid_width // lax.axis_size(DP)
    half = lax.axis_index("zh")
    weight = down_weight[0]

    part = hid_width // lax.axis_size(SHARE)
    share = lax.dynamic_slice_in_dim(weight, lax.axis_index(SHARE) * part, part, axis=0)
    share = lax.ppermute(share, "zh", [(0, 1), (1, 0)])

    expert_list = expert_ids[:, 0]
    onehot = (expert_list[:, None] == jnp.arange(experts, dtype=I32)[None, :]).astype(I32)
    row_rank = jnp.sum(onehot * (jnp.cumsum(onehot, axis=0) - 1), axis=1)
    slot_index = expert_list * slots + row_rank
    placer = (jnp.arange(tall, dtype=I32)[:, None] == slot_index[None, :]).astype(BF16)
    grad_rows = (gate_weights * out_grad.astype(F32)).astype(BF16)
    outgoing = jnp.concatenate(
        [dot(placer, grad_rows, ((1,), (0,))), dot(placer, hidden, ((1,), (0,)))], axis=1
    )
    arrived = exchange(outgoing.reshape(columns, block, -1), "y").reshape(tall, -1)
    arrived, share = lax.optimization_barrier((arrived, share))
    other_weight = lax.all_gather(share, SHARE, axis=0, tiled=True)
    grad_flat, hid_flat = arrived[:, :out_width], arrived[:, out_width:]

    full = jnp.arange(columns * halves * capacity, dtype=I32)
    compact = chooser(full // capacity * slots + full % capacity, tall)
    place = jnp.arange(hid_width, dtype=I32)
    in_quarter = place % (hid_width // xs)
    source = (
        in_quarter // (cs * strip) * (near * strip)
        + place // (hid_width // xs) * (cs * strip)
        + in_quarter % (cs * strip)
    )
    sorter = chooser(source, hid_width)
    hid_sorted = dot(dot(compact, hid_flat, ((1,), (0,))), sorter, ((1,), (1,)))
    grad_sorted = dot(compact, grad_flat, ((1,), (0,)))
    rows = full.shape[0]
    blocks = [
        jnp.concatenate(
            [
                hid_sorted[:, x * (hid_width // xs) : (x + 1) * (hid_width // xs)],
                grad_sorted[:, c * (out_width // cs) : (c + 1) * (out_width // cs)],
            ],
            axis=1,
        )
        for x in range(xs)
        for c in range(cs)
    ]
    near_rows = exchange(jnp.stack(blocks), NEAR).reshape(near * rows, -1)
    near_rows, other_weight = lax.optimization_barrier((near_rows, other_weight))
    hid_near, grad_near = near_rows[:, : hid_width // xs], near_rows[:, hid_width // xs :]
    of_half = (jnp.arange(near * rows, dtype=I32) // capacity % halves)[:, None]
    zero = jnp.zeros((), BF16)
    by_half = jnp.concatenate(
        [jnp.where(of_half == h, hid_near, zero) for h in range(halves)], axis=1
    )
    partial_grad = dot(by_half, grad_near, ((0,), (0,)))
    arrived, partial_grad = lax.optimization_barrier((arrived, partial_grad))
    parts = exchange(partial_grad.reshape(-1, strip, out_width // cs), RING)

    here = lax.axis_index("y")
    turned = lax.dynamic_slice_in_dim(
        jnp.concatenate([arrived, arrived], axis=0), here * block, tall, axis=0
    )
    grad_turned, hid_turned = turned[:, :out_width], turned[:, out_width:]
    own = (jnp.arange(tall, dtype=I32) // slots % halves)[:, None] == half
    proj = jnp.where(
        own, dot(hid_turned, weight, ((1,), (0,))), dot(hid_turned, other_weight, ((1,), (0,)))
    )
    back = jnp.where(
        own, dot(grad_turned, weight, ((1,), (1,))), dot(grad_turned, other_weight, ((1,), (1,)))
    )
    leaving = jnp.concatenate([proj, back], axis=1)
    returned = jnp.concatenate(
        [leaving[:block]]
        + [
            lax.ppermute(
                leaving[k * block : (k + 1) * block],
                "y",
                [(y, (y + k) % columns) for y in range(columns)],
            )
            for k in range(1, columns)
        ],
        axis=0,
    )
    turns = jnp.mod(here - expert_list // halves, columns)
    fetch_index = turns * block + expert_list % halves * slots + row_rank
    fetcher = (jnp.arange(tall, dtype=I32)[:, None] == fetch_index[None, :]).astype(BF16)
    projected = dot(fetcher, returned[:, :out_width], ((0,), (0,)), F32)
    layer_out = (gate_weights * projected).astype(BF16)
    gate_grad = jnp.sum(out_grad.astype(F32) * projected, axis=1, keepdims=True)
    hidden_grad = dot(fetcher, returned[:, out_width:], ((0,), (0,)))

    summed = jnp.sum(parts.reshape(-1, cs, strip, out_width // cs).astype(F32), axis=0)
    weight_grad = summed.swapaxes(0, 1).reshape(strip, out_width)
    return (layer_out, hidden_grad, gate_grad, weight_grad[None])


def solution(mesh):
    fine = Mesh(mesh.devices.reshape(4, 2, 4, 2, 8, 2), DP + EXP)
    tokens = P(DP + EXP, None)
    return jax.shard_map(
        shards,
        mesh=fine,
        in_specs=(tokens, tokens, tokens, P(EXP, None, None), tokens),
        out_specs=(tokens, tokens, tokens, P(EXP, DP, None)),
        check_vma=False,
    )
```

```python
import jax
import jax.numpy as jnp
from jax import lax
from jax.sharding import Mesh, PartitionSpec as P

F32, BF16, I32 = jnp.float32, jnp.bfloat16, jnp.int32
LINE = ("zq", "zp")
DP = LINE + ("x", "c")
EXP = ("y", "zh")
NEAR = ("x", "c")
SHARE = ("zp", "x")
RING = ("zh",) + LINE + ("c",)


def exchange(blocks, axes):
    return lax.all_to_all(blocks, axes, split_axis=0, concat_axis=0, tiled=True)


def dot(a, b, dims, out=BF16):
    return lax.dot_general(a, b, (dims, ((), ())), preferred_element_type=F32).astype(out)


def chooser(wanted, count):
    return (wanted[:, None] == jnp.arange(count, dtype=I32)[None, :]).astype(BF16)


def shards(hidden, expert_ids, gate_weights, down_weight, out_grad):
    tok_rows, hid_width = hidden.shape
    out_width = out_grad.shape[1]
    columns, halves = lax.axis_size("y"), lax.axis_size("zh")
    experts = columns * halves
    xs, cs, near, lines = (lax.axis_size(axes) for axes in ("x", "c", NEAR, LINE))
    capacity = 5 * tok_rows // (4 * experts)
    slots = capacity + -capacity % 4
    block = halves * slots
    tall = columns * block
    strip = hid_width // lax.axis_size(DP)
    half = lax.axis_index("zh")
    weight = down_weight[0]

    core = lax.axis_index("c")
    part = hid_width // cs // lax.axis_size(SHARE)
    start = core * (hid_width // cs) + lax.axis_index(SHARE) * part
    share = lax.dynamic_slice_in_dim(weight, start, part, axis=0)
    share = lax.ppermute(share, "zh", [(0, 1), (1, 0)])

    expert_list = expert_ids[:, 0]
    onehot = (expert_list[:, None] == jnp.arange(experts, dtype=I32)[None, :]).astype(I32)
    row_rank = jnp.sum(onehot * (jnp.cumsum(onehot, axis=0) - 1), axis=1)
    slot_index = expert_list * slots + row_rank
    placer = (jnp.arange(tall, dtype=I32)[:, None] == slot_index[None, :]).astype(BF16)
    grad_rows = (gate_weights * out_grad.astype(F32)).astype(BF16)
    outgoing = jnp.concatenate(
        [dot(placer, grad_rows, ((1,), (0,))), dot(placer, hidden, ((1,), (0,)))], axis=1
    )
    arrived = exchange(outgoing.reshape(columns, block, -1), "y").reshape(tall, -1)
    arrived, share = lax.optimization_barrier((arrived, share))
    near_weight = lax.all_gather(share, SHARE, axis=0, tiled=True)
    grad_flat, hid_flat = arrived[:, :out_width], arrived[:, out_width:]

    full = jnp.arange(columns * halves * capacity, dtype=I32)
    compact = chooser(full // capacity * slots + full % capacity, tall)
    place = jnp.arange(hid_width, dtype=I32)
    in_quarter = place % (hid_width // xs)
    source = (
        in_quarter // (cs * strip) * (near * strip)
        + place // (hid_width // xs) * (cs * strip)
        + in_quarter % (cs * strip)
    )
    sorter = chooser(source, hid_width)
    hid_sorted = dot(dot(compact, hid_flat, ((1,), (0,))), sorter, ((1,), (1,)))
    grad_sorted = dot(compact, grad_flat, ((1,), (0,)))
    rows = full.shape[0]
    blocks = [
        jnp.concatenate(
            [
                hid_sorted[:, x * (hid_width // xs) : (x + 1) * (hid_width // xs)],
                grad_sorted[:, c * (out_width // cs) : (c + 1) * (out_width // cs)],
            ],
            axis=1,
        )
        for x in range(xs)
        for c in range(cs)
    ]
    near_rows = exchange(jnp.stack(blocks), NEAR).reshape(near * rows, -1)
    near_rows, near_weight = lax.optimization_barrier((near_rows, near_weight))
    far_weight = lax.ppermute(near_weight, "c", [(0, 1), (1, 0)])
    hid_near, grad_near = near_rows[:, : hid_width // xs], near_rows[:, hid_width // xs :]
    of_half = (jnp.arange(near * rows, dtype=I32) // capacity % halves)[:, None]
    zero = jnp.zeros((), BF16)
    by_half = jnp.concatenate(
        [jnp.where(of_half == h, hid_near, zero) for h in range(halves)], axis=1
    )
    partial_grad = dot(by_half, grad_near, ((0,), (0,)))
    arrived, partial_grad = lax.optimization_barrier((arrived, partial_grad))
    parts = exchange(partial_grad.reshape(-1, strip, out_width // cs), RING)

    here = lax.axis_index("y")
    turned = lax.dynamic_slice_in_dim(
        jnp.concatenate([arrived, arrived], axis=0), here * block, tall, axis=0
    )
    grad_turned, hid_turned = turned[:, :out_width], turned[:, out_width:]
    own = (jnp.arange(tall, dtype=I32) // slots % halves)[:, None] == half
    first = core == 0
    lower, upper = hid_turned[:, : hid_width // cs], hid_turned[:, hid_width // cs :]
    proj_other = dot(jnp.where(first, lower, upper), near_weight, ((1,), (0,)), F32) + dot(
        jnp.where(first, upper, lower), far_weight, ((1,), (0,)), F32
    )
    proj = jnp.where(own, dot(hid_turned, weight, ((1,), (0,))), proj_other.astype(BF16))
    back_near = dot(grad_turned, near_weight, ((1,), (1,)))
    back_far = dot(grad_turned, far_weight, ((1,), (1,)))
    back_other = jnp.concatenate(
        [jnp.where(first, back_near, back_far), jnp.where(first, back_far, back_near)], axis=1
    )
    back = jnp.where(own, dot(grad_turned, weight, ((1,), (1,))), back_other)
    leaving = jnp.concatenate([proj, back], axis=1)
    returned = jnp.concatenate(
        [leaving[:block]]
        + [
            lax.ppermute(
                leaving[k * block : (k + 1) * block],
                "y",
                [(y, (y + k) % columns) for y in range(columns)],
            )
            for k in range(1, columns)
        ],
        axis=0,
    )
    turns = jnp.mod(here - expert_list // halves, columns)
    fetch_index = turns * block + expert_list % halves * slots + row_rank
    fetcher = (jnp.arange(tall, dtype=I32)[:, None] == fetch_index[None, :]).astype(BF16)
    projected = dot(fetcher, returned[:, :out_width], ((0,), (0,)), F32)
    layer_out = (gate_weights * projected).astype(BF16)
    gate_grad = jnp.sum(out_grad.astype(F32) * projected, axis=1, keepdims=True)
    hidden_grad = dot(fetcher, returned[:, out_width:], ((0,), (0,)))

    summed = jnp.sum(parts.reshape(-1, cs, strip, out_width // cs).astype(F32), axis=0)
    weight_grad = summed.swapaxes(0, 1).reshape(strip, out_width)
    return (layer_out, hidden_grad, gate_grad, weight_grad[None])


def solution(mesh):
    fine = Mesh(mesh.devices.reshape(4, 2, 4, 2, 8, 2), DP + EXP)
    tokens = P(DP + EXP, None)
    return jax.shard_map(
        shards,
        mesh=fine,
        in_specs=(tokens, tokens, tokens, P(EXP, None, None), tokens),
        out_specs=(tokens, tokens, tokens, P(EXP, DP, None)),
        check_vma=False,
    )
```

```python
import jax
import jax.numpy as jnp
from jax import lax
from jax.sharding import Mesh, PartitionSpec as P

F32, BF16, I32 = jnp.float32, jnp.bfloat16, jnp.int32
DP = ("zl", "x", "c")
EXP = ("y", "zh")
NEAR = ("x", "c")
LINE = ("zl", "c")


def exchange(blocks, axes):
    return lax.all_to_all(blocks, axes, split_axis=0, concat_axis=0, tiled=True)


def dot(a, b, dims, out=BF16):
    return lax.dot_general(a, b, (dims, ((), ())), preferred_element_type=F32).astype(out)


def chooser(wanted, count):
    return (wanted[:, None] == jnp.arange(count, dtype=I32)[None, :]).astype(BF16)


def shards(hidden, expert_ids, gate_weights, down_weight, out_grad):
    tok_rows, hid_width = hidden.shape
    out_width = out_grad.shape[1]
    experts = lax.axis_size(EXP)
    xs, cs, near = (lax.axis_size(axes) for axes in ("x", "c", NEAR))
    capacity = 5 * tok_rows // (4 * experts)
    rows = experts * capacity
    block = 16 * (-(-(capacity + (capacity + 1) // 2) // 16))
    tall = experts * block
    strip = hid_width // lax.axis_size(DP)
    weight = down_weight[0]

    def wide_place(expert, rank):
        return expert * block + rank

    def pair_place(expert, rank):
        return expert * block + capacity + rank // 2

    def paired(narrow, odd):
        zero = jnp.zeros((), narrow.dtype)
        return jnp.concatenate(
            [jnp.where(odd, zero, narrow), jnp.where(odd, narrow, zero)], axis=1
        )

    def unpaired(wide, odd):
        return jnp.where(odd, wide[:, hid_width:], wide[:, :hid_width])

    expert_list = expert_ids[:, 0]
    onehot = (expert_list[:, None] == jnp.arange(experts, dtype=I32)[None, :]).astype(I32)
    row_rank = jnp.sum(onehot * (jnp.cumsum(onehot, axis=0) - 1), axis=1)
    odd = (row_rank % 2 == 1)[:, None]
    places = jnp.concatenate(
        [wide_place(expert_list, row_rank), pair_place(expert_list, row_rank)]
    )
    placer = (jnp.arange(tall, dtype=I32)[:, None] == places[None, :]).astype(BF16)
    grad_rows = (gate_weights * out_grad.astype(F32)).astype(BF16)
    outgoing = dot(
        placer, jnp.concatenate([grad_rows, paired(hidden, odd)], axis=0), ((1,), (0,))
    )
    arrived = exchange(outgoing.reshape(experts, block, -1), EXP).reshape(tall, -1)
    full = jnp.arange(rows, dtype=I32)
    source, rank = full // capacity, full % capacity
    full_odd = (rank % 2 == 1)[:, None]
    picker = chooser(jnp.concatenate([wide_place(source, rank), pair_place(source, rank)]), tall)
    picked = dot(picker, arrived, ((1,), (0,)))
    grad_flat, hid_flat = picked[:rows], unpaired(picked[rows:], full_odd)

    quarter, half = hid_width // xs, out_width // cs
    place = jnp.arange(hid_width, dtype=I32)
    in_quarter = place % quarter
    column = (
        in_quarter // (cs * strip) * (near * strip)
        + place // quarter * (cs * strip)
        + in_quarter % (cs * strip)
    )
    hid_sorted = dot(hid_flat, chooser(column, hid_width), ((1,), (1,)))
    blocks = [
        jnp.concatenate(
            [
                hid_sorted[:, x * quarter : (x + 1) * quarter],
                grad_flat[:, c * half : (c + 1) * half],
            ],
            axis=1,
        )
        for x in range(xs)
        for c in range(cs)
    ]
    near_rows = exchange(jnp.stack(blocks), NEAR).reshape(near * rows, -1)

    proj = dot(hid_flat, weight, ((1,), (0,)))
    back = dot(grad_flat, weight, ((1,), (1,)))
    leaving = dot(
        picker, jnp.concatenate([proj, paired(back, full_odd)], axis=0), ((0,), (0,))
    )
    leaving, near_rows = lax.optimization_barrier((leaving, near_rows))
    returned = exchange(leaving.reshape(experts, block, -1), EXP).reshape(tall, -1)
    partial_grad = dot(near_rows[:, :quarter], near_rows[:, quarter:], ((0,), (0,)))

    returned, partial_grad = lax.optimization_barrier((returned, partial_grad))
    parts = exchange(partial_grad.reshape(-1, strip, half), LINE)
    fetched = dot(placer, returned, ((0,), (0,)), F32)
    projected = fetched[:tok_rows]
    layer_out = (gate_weights * projected).astype(BF16)
    gate_grad = jnp.sum(out_grad.astype(F32) * projected, axis=1, keepdims=True)
    hidden_grad = unpaired(fetched[tok_rows:], odd).astype(BF16)
    summed = jnp.sum(parts.reshape(-1, cs, strip, half).astype(F32), axis=0)
    weight_grad = summed.swapaxes(0, 1).reshape(strip, out_width)
    return (layer_out, hidden_grad, gate_grad, weight_grad[None])


def solution(mesh):
    fine = Mesh(mesh.devices.reshape(8, 4, 2, 8, 2), DP + EXP)
    tokens = P(DP + EXP, None)
    return jax.shard_map(
        shards,
        mesh=fine,
        in_specs=(tokens, tokens, tokens, P(EXP, None, None), tokens),
        out_specs=(tokens, tokens, tokens, P(EXP, DP, None)),
        check_vma=False,
    )
```

```python
import functools

import jax
import jax.numpy as jnp
from jax import lax
from jax.experimental import pallas as pl
from jax.experimental.pallas import tpu as pltpu
from jax.sharding import Mesh, PartitionSpec as P

F32, BF16, I32 = jnp.float32, jnp.bfloat16, jnp.int32
LINE = ("zq", "zp")
DP = LINE + ("x", "c")
EXP = ("y", "zh")
NEAR = ("x", "c")
SHARE = ("zp", "x", "c")
RING = ("zh",) + LINE + ("c",)


def exchange(blocks, axes):
    return lax.all_to_all(blocks, axes, split_axis=0, concat_axis=0, tiled=True)


def dot(a, b, dims, out=BF16):
    return lax.dot_general(a, b, (dims, ((), ())), preferred_element_type=F32).astype(out)


def pack_kernel(capacity, slots, strip, xs, cs, hid_width, arrived, blocks):
    tall, width = arrived.shape
    rows = blocks.shape[1]
    quarter = hid_width // xs
    half = (width - hid_width) // cs
    full = lax.broadcasted_iota(I32, (rows, tall), 0)
    wanted = full // capacity * slots + full % capacity
    compact = (wanted == lax.broadcasted_iota(I32, (rows, tall), 1)).astype(BF16)
    kept = dot(compact, arrived[...], ((1,), (0,)))
    group = cs * strip
    place = lax.broadcasted_iota(I32, (hid_width, hid_width), 0)
    target = place // group % xs * quarter + place // (group * xs) * group + place % group
    sorter = (target == lax.broadcasted_iota(I32, (hid_width, hid_width), 1)).astype(BF16)
    hid = dot(kept[:, width - hid_width :], sorter, ((1,), (0,)))
    for x in range(xs):
        for c in range(cs):
            blocks[x * cs + c, :, :quarter] = hid[:, x * quarter : (x + 1) * quarter]
            blocks[x * cs + c, :, quarter:] = kept[:, c * half : (c + 1) * half]


def shards(hidden, expert_ids, gate_weights, down_weight, out_grad):
    tok_rows, hid_width = hidden.shape
    out_width = out_grad.shape[1]
    columns, halves = lax.axis_size("y"), lax.axis_size("zh")
    experts = columns * halves
    xs, cs, near = (lax.axis_size(axes) for axes in ("x", "c", NEAR))
    capacity = 5 * tok_rows // (4 * experts)
    slots = capacity + -capacity % 4
    block = halves * slots
    tall = columns * block
    strip = hid_width // lax.axis_size(DP)
    half = lax.axis_index("zh")
    weight = down_weight[0]

    part = hid_width // lax.axis_size(SHARE)
    start = lax.axis_index(SHARE) * part
    share = lax.dynamic_slice_in_dim(weight, start, part, axis=0)
    share = lax.ppermute(share, "zh", [(0, 1), (1, 0)])

    expert_list = expert_ids[:, 0]
    onehot = (expert_list[:, None] == jnp.arange(experts, dtype=I32)[None, :]).astype(I32)
    row_rank = jnp.sum(onehot * (jnp.cumsum(onehot, axis=0) - 1), axis=1)
    slot_index = expert_list * slots + row_rank
    placer = (jnp.arange(tall, dtype=I32)[:, None] == slot_index[None, :]).astype(BF16)
    grad_rows = (gate_weights * out_grad.astype(F32)).astype(BF16)
    outgoing = jnp.concatenate(
        [dot(placer, grad_rows, ((1,), (0,))), dot(placer, hidden, ((1,), (0,)))], axis=1
    )
    arrived = exchange(outgoing.reshape(columns, block, -1), "y").reshape(tall, -1)
    arrived, share = lax.optimization_barrier((arrived, share))
    beside = lax.ppermute(share, "zp", [(0, 1), (1, 0)])

    rows = experts * capacity
    near_rows = exchange(
        pl.pallas_call(
            functools.partial(pack_kernel, capacity, slots, strip, xs, cs, hid_width),
            out_shape=jax.ShapeDtypeStruct(
                (near, rows, hid_width // xs + out_width // cs), BF16
            ),
            compiler_params=pltpu.CompilerParams(vmem_limit_bytes=40 * 2**20),
            cost_estimate=pl.CostEstimate(
                flops=2 * rows * (tall * (hid_width + out_width) + hid_width**2),
                bytes_accessed=8 * 2**20,
                transcendentals=0,
            ),
        )(arrived),
        NEAR,
    ).reshape(near * rows, -1)
    near_rows, share, beside = lax.optimization_barrier((near_rows, share, beside))
    even = lax.axis_index("zp") == 0
    pair = jnp.stack([jnp.where(even, share, beside), jnp.where(even, beside, share)])
    other_weight = lax.all_gather(pair, NEAR, axis=1, tiled=True).reshape(hid_width, -1)
    hid_near, grad_near = near_rows[:, : hid_width // xs], near_rows[:, hid_width // xs :]
    of_half = (jnp.arange(near * rows, dtype=I32) // capacity % halves)[:, None]
    zero = jnp.zeros((), BF16)
    by_half = jnp.concatenate(
        [jnp.where(of_half == h, hid_near, zero) for h in range(halves)], axis=1
    )
    partial_grad = dot(by_half, grad_near, ((0,), (0,)))
    parts = exchange(partial_grad.reshape(-1, strip, out_width // cs), RING)

    grad_flat, hid_flat = arrived[:, :out_width], arrived[:, out_width:]
    own = (jnp.arange(tall, dtype=I32) // slots % halves)[:, None] == half
    proj = jnp.where(
        own, dot(hid_flat, weight, ((1,), (0,))), dot(hid_flat, other_weight, ((1,), (0,)))
    )
    back = jnp.where(
        own, dot(grad_flat, weight, ((1,), (1,))), dot(grad_flat, other_weight, ((1,), (1,)))
    )
    leaving = jnp.concatenate([proj, back], axis=1)
    leaving, parts = lax.optimization_barrier((leaving, parts))
    returned = exchange(leaving.reshape(columns, block, -1), "y").reshape(tall, -1)
    projected = dot(placer, returned[:, :out_width], ((0,), (0,)), F32)
    layer_out = (gate_weights * projected).astype(BF16)
    gate_grad = jnp.sum(out_grad.astype(F32) * projected, axis=1, keepdims=True)
    hidden_grad = dot(placer, returned[:, out_width:], ((0,), (0,)))

    summed = jnp.sum(parts.reshape(-1, cs, strip, out_width // cs).astype(F32), axis=0)
    weight_grad = summed.swapaxes(0, 1).reshape(strip, out_width)
    return (layer_out, hidden_grad, gate_grad, weight_grad[None])


def solution(mesh):
    fine = Mesh(mesh.devices.reshape(4, 2, 4, 2, 8, 2), DP + EXP)
    tokens = P(DP + EXP, None)
    return jax.shard_map(
        shards,
        mesh=fine,
        in_specs=(tokens, tokens, tokens, P(EXP, None, None), tokens),
        out_specs=(tokens, tokens, tokens, P(EXP, DP, None)),
        check_vma=False,
    )
```

```python
import functools

import jax
import jax.numpy as jnp
from jax import lax
from jax.experimental import pallas as pl
from jax.experimental.pallas import tpu as pltpu
from jax.sharding import Mesh, PartitionSpec as P

F32, BF16, I32 = jnp.float32, jnp.bfloat16, jnp.int32
LINE = ("zq", "zp")
DP = LINE + ("x", "c")
EXP = ("y", "zh")
NEAR = ("x", "c")
SHARE = ("zp", "x", "c")
RING = ("zh",) + LINE


def exchange(blocks, axes):
    return lax.all_to_all(blocks, axes, split_axis=0, concat_axis=0, tiled=True)


def dot(a, b, dims, out=BF16):
    return lax.dot_general(a, b, (dims, ((), ())), preferred_element_type=F32).astype(out)


def pack_kernel(capacity, slots, strip, xs, cs, hid_width, arrived, blocks):
    tall, width = arrived.shape
    rows = blocks.shape[1]
    quarter = hid_width // xs
    half = (width - hid_width) // cs
    full = lax.broadcasted_iota(I32, (rows, tall), 0)
    wanted = full // capacity * slots + full % capacity
    compact = (wanted == lax.broadcasted_iota(I32, (rows, tall), 1)).astype(BF16)
    kept = dot(compact, arrived[...], ((1,), (0,)))
    group = cs * strip
    place = lax.broadcasted_iota(I32, (hid_width, hid_width), 0)
    target = place // group % xs * quarter + place // (group * xs) * group + place % group
    sorter = (target == lax.broadcasted_iota(I32, (hid_width, hid_width), 1)).astype(BF16)
    hid = dot(kept[:, width - hid_width :], sorter, ((1,), (0,)))
    for x in range(xs):
        for c in range(cs):
            blocks[x * cs + c, :, :quarter] = hid[:, x * quarter : (x + 1) * quarter]
            blocks[x * cs + c, :, quarter:] = kept[:, c * half : (c + 1) * half]


def shards(hidden, expert_ids, gate_weights, down_weight, out_grad):
    tok_rows, hid_width = hidden.shape
    out_width = out_grad.shape[1]
    columns, halves = lax.axis_size("y"), lax.axis_size("zh")
    experts = columns * halves
    xs, cs, near = (lax.axis_size(axes) for axes in ("x", "c", NEAR))
    capacity = 5 * tok_rows // (4 * experts)
    slots = capacity + -capacity % 4
    block = halves * slots
    tall = columns * block
    strip = hid_width // lax.axis_size(DP)
    half = lax.axis_index("zh")
    weight = down_weight[0]

    part = hid_width // lax.axis_size(SHARE)
    start = lax.axis_index(SHARE) * part
    share = lax.dynamic_slice_in_dim(weight, start, part, axis=0)
    share = lax.ppermute(share, "zh", [(0, 1), (1, 0)])

    expert_list = expert_ids[:, 0]
    onehot = (expert_list[:, None] == jnp.arange(experts, dtype=I32)[None, :]).astype(I32)
    row_rank = jnp.sum(onehot * (jnp.cumsum(onehot, axis=0) - 1), axis=1)
    slot_index = expert_list * slots + row_rank
    placer = (jnp.arange(tall, dtype=I32)[:, None] == slot_index[None, :]).astype(BF16)
    grad_rows = (gate_weights * out_grad.astype(F32)).astype(BF16)
    outgoing = jnp.concatenate(
        [dot(placer, grad_rows, ((1,), (0,))), dot(placer, hidden, ((1,), (0,)))], axis=1
    )
    arrived = exchange(outgoing.reshape(columns, block, -1), "y").reshape(tall, -1)
    arrived, share = lax.optimization_barrier((arrived, share))
    beside = lax.ppermute(share, "zp", [(0, 1), (1, 0)])

    rows = experts * capacity
    near_rows = exchange(
        pl.pallas_call(
            functools.partial(pack_kernel, capacity, slots, strip, xs, cs, hid_width),
            out_shape=jax.ShapeDtypeStruct(
                (near, rows, hid_width // xs + out_width // cs), BF16
            ),
            compiler_params=pltpu.CompilerParams(vmem_limit_bytes=40 * 2**20),
            cost_estimate=pl.CostEstimate(
                flops=2 * rows * (tall * (hid_width + out_width) + hid_width**2),
                bytes_accessed=8 * 2**20,
                transcendentals=0,
            ),
        )(arrived),
        NEAR,
    ).reshape(near * rows, -1)
    near_rows, share, beside = lax.optimization_barrier((near_rows, share, beside))
    even = lax.axis_index("zp") == 0
    pair = jnp.stack([jnp.where(even, share, beside), jnp.where(even, beside, share)])
    other_weight = lax.all_gather(pair, NEAR, axis=1, tiled=True).reshape(hid_width, -1)
    hid_near, grad_near = near_rows[:, : hid_width // xs], near_rows[:, hid_width // xs :]
    of_half = (jnp.arange(near * rows, dtype=I32) // capacity % halves)[:, None]
    zero = jnp.zeros((), BF16)
    by_half = jnp.concatenate(
        [jnp.where(of_half == h, hid_near, zero) for h in range(halves)], axis=1
    )
    partial_grad = dot(by_half, grad_near, ((0,), (0,)), F32)
    ring_sum = lax.psum_scatter(partial_grad, RING, scatter_dimension=0, tiled=True)

    full = jnp.arange(columns * capacity, dtype=I32)
    origin, rank = full // capacity, full % capacity
    odd = (rank % 2 == 1)[:, None]
    back_block = 16 * (-(-(capacity + (capacity + 1) // 2) // 16))
    short = columns * back_block

    def products(which, matrix, arrived):
        wanted = origin * block + which * slots + rank
        chosen = (wanted[:, None] == jnp.arange(tall, dtype=I32)[None, :]).astype(BF16)
        picked = dot(chosen, arrived, ((1,), (0,)))
        proj = dot(picked[:, out_width:], matrix, ((1,), (0,)))
        back = dot(picked[:, :out_width], matrix, ((1,), (1,)))
        zero = jnp.zeros((), BF16)
        pairs = jnp.concatenate(
            [jnp.where(odd, zero, back), jnp.where(odd, back, zero)], axis=1
        )
        spots = origin * back_block
        spots = jnp.concatenate([spots + rank, spots + capacity + rank // 2])
        spread = (jnp.arange(short, dtype=I32)[:, None] == spots[None, :]).astype(BF16)
        return dot(spread, jnp.concatenate([proj, pairs], axis=0), ((1,), (0,)))

    own_leaving, _ = lax.optimization_barrier((products(half, weight, arrived), partial_grad))
    own_back = exchange(own_leaving.reshape(columns, back_block, -1), "y").reshape(short, -1)
    arrived, own_back = lax.optimization_barrier((arrived, own_back))
    other_leaving = products(1 - half, other_weight, arrived)
    other_back = exchange(other_leaving.reshape(columns, back_block, -1), "y")
    other_back, ring_sum = lax.optimization_barrier((other_back.reshape(short, -1), ring_sum))
    returned = jnp.concatenate([own_back, other_back], axis=0)
    seat = jnp.where(expert_list % halves == half, 0, short) + expert_list // halves * back_block
    seats = jnp.concatenate([seat + row_rank, seat + capacity + row_rank // 2])
    fetcher = (jnp.arange(2 * short, dtype=I32)[:, None] == seats[None, :]).astype(BF16)
    fetched = dot(fetcher, returned, ((0,), (0,)), F32)
    projected = fetched[:tok_rows]
    hidden_grad = jnp.where(
        (row_rank % 2 == 1)[:, None],
        fetched[tok_rows:, hid_width:],
        fetched[tok_rows:, :hid_width],
    ).astype(BF16)
    layer_out = (gate_weights * projected).astype(BF16)
    gate_grad = jnp.sum(out_grad.astype(F32) * projected, axis=1, keepdims=True)

    core = lax.axis_index("c")
    first = core == 0
    kept = lax.dynamic_slice_in_dim(ring_sum, core * strip, strip, axis=0)
    given = lax.dynamic_slice_in_dim(ring_sum, (1 - core) * strip, strip, axis=0)
    taken = lax.ppermute(given, "c", [(0, 1), (1, 0)])
    weight_grad = jnp.concatenate(
        [jnp.where(first, kept, taken), jnp.where(first, taken, kept)], axis=1
    )
    return (layer_out, hidden_grad, gate_grad, weight_grad[None])


def solution(mesh):
    fine = Mesh(mesh.devices.reshape(4, 2, 4, 2, 8, 2), DP + EXP)
    tokens = P(DP + EXP, None)
    return jax.shard_map(
        shards,
        mesh=fine,
        in_specs=(tokens, tokens, tokens, P(EXP, None, None), tokens),
        out_specs=(tokens, tokens, tokens, P(EXP, DP, None)),
        check_vma=False,
    )
```

```python
import functools

import jax
import jax.numpy as jnp
from jax import lax
from jax.experimental import pallas as pl
from jax.experimental.pallas import tpu as pltpu
from jax.sharding import Mesh, PartitionSpec as P

F32, BF16, I32 = jnp.float32, jnp.bfloat16, jnp.int32
LINE = ("zq", "zp")
DP = LINE + ("x", "c")
EXP = ("y", "zh")
NEAR = ("x", "c")
GROUP = ("zp",) + NEAR
SHARE = ("zp", "x", "c")
RING = ("zh", "zq")


def exchange(blocks, axes):
    return lax.all_to_all(blocks, axes, split_axis=0, concat_axis=0, tiled=True)


def dot(a, b, dims, out=BF16):
    return lax.dot_general(a, b, (dims, ((), ())), preferred_element_type=F32).astype(out)


def pack_kernel(capacity, slots, strip, zs, xs, cs, hid_width, arrived, blocks):
    tall, width = arrived.shape
    rows = blocks.shape[1]
    quarter = hid_width // xs
    part = (width - hid_width) // (zs * cs)
    full = lax.broadcasted_iota(I32, (rows, tall), 0)
    wanted = full // capacity * slots + full % capacity
    compact = (wanted == lax.broadcasted_iota(I32, (rows, tall), 1)).astype(BF16)
    kept = dot(compact, arrived[...], ((1,), (0,)))
    group = cs * strip
    place = lax.broadcasted_iota(I32, (hid_width, hid_width), 0)
    target = place // group % xs * quarter + place // (group * xs) * group + place % group
    sorter = (target == lax.broadcasted_iota(I32, (hid_width, hid_width), 1)).astype(BF16)
    hid = dot(kept[:, width - hid_width :], sorter, ((1,), (0,)))
    for z in range(zs):
        for x in range(xs):
            for c in range(cs):
                block, wide = (z * xs + x) * cs + c, z * cs + c
                blocks[block, :, :quarter] = hid[:, x * quarter : (x + 1) * quarter]
                blocks[block, :, quarter:] = kept[:, wide * part : (wide + 1) * part]


def shards(hidden, expert_ids, gate_weights, down_weight, out_grad):
    tok_rows, hid_width = hidden.shape
    out_width = out_grad.shape[1]
    columns, halves = lax.axis_size("y"), lax.axis_size("zh")
    experts = columns * halves
    zs, xs, cs, group = (lax.axis_size(axes) for axes in ("zp", "x", "c", GROUP))
    capacity = 5 * tok_rows // (4 * experts)
    slots = capacity + -capacity % 4
    block = halves * slots
    tall = columns * block
    strip = hid_width // lax.axis_size(DP)
    half = lax.axis_index("zh")
    weight = down_weight[0]

    part = hid_width // lax.axis_size(SHARE)
    start = lax.axis_index(SHARE) * part
    share = lax.dynamic_slice_in_dim(weight, start, part, axis=0)
    share = lax.ppermute(share, "zh", [(0, 1), (1, 0)])

    expert_list = expert_ids[:, 0]
    onehot = (expert_list[:, None] == jnp.arange(experts, dtype=I32)[None, :]).astype(I32)
    row_rank = jnp.sum(onehot * (jnp.cumsum(onehot, axis=0) - 1), axis=1)
    slot_index = expert_list * slots + row_rank
    placer = (jnp.arange(tall, dtype=I32)[:, None] == slot_index[None, :]).astype(BF16)
    grad_rows = (gate_weights * out_grad.astype(F32)).astype(BF16)
    outgoing = jnp.concatenate(
        [dot(placer, grad_rows, ((1,), (0,))), dot(placer, hidden, ((1,), (0,)))], axis=1
    )
    arrived = exchange(outgoing.reshape(columns, block, -1), "y").reshape(tall, -1)
    arrived, share = lax.optimization_barrier((arrived, share))
    beside = lax.ppermute(share, "zp", [(0, 1), (1, 0)])

    rows = experts * capacity
    near_rows = exchange(
        pl.pallas_call(
            functools.partial(pack_kernel, capacity, slots, strip, zs, xs, cs, hid_width),
            out_shape=jax.ShapeDtypeStruct(
                (group, rows, hid_width // xs + out_width // (zs * cs)), BF16
            ),
            compiler_params=pltpu.CompilerParams(vmem_limit_bytes=40 * 2**20),
            cost_estimate=pl.CostEstimate(
                flops=2 * rows * (tall * (hid_width + out_width) + hid_width**2),
                bytes_accessed=8 * 2**20,
                transcendentals=0,
            ),
        )(arrived),
        GROUP,
    ).reshape(group * rows, -1)
    near_rows, share, beside = lax.optimization_barrier((near_rows, share, beside))
    even = lax.axis_index("zp") == 0
    pair = jnp.stack([jnp.where(even, share, beside), jnp.where(even, beside, share)])
    other_weight = lax.all_gather(pair, NEAR, axis=1, tiled=True).reshape(hid_width, -1)
    hid_near, grad_near = near_rows[:, : hid_width // xs], near_rows[:, hid_width // xs :]
    of_half = (jnp.arange(group * rows, dtype=I32) // capacity % halves)[:, None]
    zero = jnp.zeros((), BF16)
    by_half = jnp.concatenate(
        [jnp.where(of_half == h, hid_near, zero) for h in range(halves)], axis=1
    )
    partial_grad = dot(by_half, grad_near, ((0,), (0,)), F32)
    ring_sum = lax.psum_scatter(partial_grad, RING, scatter_dimension=0, tiled=True)

    full = jnp.arange(columns * capacity, dtype=I32)
    origin, rank = full // capacity, full % capacity
    odd = (rank % 2 == 1)[:, None]
    back_block = 16 * (-(-(capacity + (capacity + 1) // 2) // 16))
    short = columns * back_block

    def products(which, matrix, arrived):
        wanted = origin * block + which * slots + rank
        chosen = (wanted[:, None] == jnp.arange(tall, dtype=I32)[None, :]).astype(BF16)
        picked = dot(chosen, arrived, ((1,), (0,)))
        proj = dot(picked[:, out_width:], matrix, ((1,), (0,)))
        back = dot(picked[:, :out_width], matrix, ((1,), (1,)))
        zero = jnp.zeros((), BF16)
        pairs = jnp.concatenate(
            [jnp.where(odd, zero, back), jnp.where(odd, back, zero)], axis=1
        )
        spots = origin * back_block
        spots = jnp.concatenate([spots + rank, spots + capacity + rank // 2])
        spread = (jnp.arange(short, dtype=I32)[:, None] == spots[None, :]).astype(BF16)
        return dot(spread, jnp.concatenate([proj, pairs], axis=0), ((1,), (0,)))

    own_leaving, _ = lax.optimization_barrier((products(half, weight, arrived), partial_grad))
    own_back = exchange(own_leaving.reshape(columns, back_block, -1), "y").reshape(short, -1)
    arrived, own_back = lax.optimization_barrier((arrived, own_back))
    other_leaving = products(1 - half, other_weight, arrived)
    other_leaving, ring_sum = lax.optimization_barrier((other_leaving, ring_sum))
    other_back = exchange(other_leaving.reshape(columns, back_block, -1), "y")
    other_back = other_back.reshape(short, -1)

    members = zs * cs
    seat = lax.axis_index(("zp", "c"))
    held = [
        lax.dynamic_slice_in_dim(ring_sum, (seat ^ k) * strip, strip, axis=0)
        for k in range(members)
    ]
    held = [held[0]] + [
        lax.ppermute(held[k], ("zp", "c"), [(i, i ^ k) for i in range(members)])
        for k in range(1, members)
    ]
    quarters = []
    for p in range(members):
        chosen = held[0]
        for k in range(1, members):
            chosen = jnp.where((seat ^ k) == p, held[k], chosen)
        quarters.append(chosen)
    weight_grad = jnp.concatenate(quarters, axis=1)
    other_back, weight_grad = lax.optimization_barrier((other_back, weight_grad))

    returned = jnp.concatenate([own_back, other_back], axis=0)
    base = jnp.where(expert_list % halves == half, 0, short) + expert_list // halves * back_block
    seats = jnp.concatenate([base + row_rank, base + capacity + row_rank // 2])
    fetcher = (jnp.arange(2 * short, dtype=I32)[:, None] == seats[None, :]).astype(BF16)
    fetched = dot(fetcher, returned, ((0,), (0,)), F32)
    projected = fetched[:tok_rows]
    hidden_grad = jnp.where(
        (row_rank % 2 == 1)[:, None],
        fetched[tok_rows:, hid_width:],
        fetched[tok_rows:, :hid_width],
    ).astype(BF16)
    layer_out = (gate_weights * projected).astype(BF16)
    gate_grad = jnp.sum(out_grad.astype(F32) * projected, axis=1, keepdims=True)

    return (layer_out, hidden_grad, gate_grad, weight_grad[None])


def solution(mesh):
    fine = Mesh(mesh.devices.reshape(4, 2, 4, 2, 8, 2), DP + EXP)
    tokens = P(DP + EXP, None)
    return jax.shard_map(
        shards,
        mesh=fine,
        in_specs=(tokens, tokens, tokens, P(EXP, None, None), tokens),
        out_specs=(tokens, tokens, tokens, P(EXP, DP, None)),
        check_vma=False,
    )
```

```python
import functools

import jax
import jax.numpy as jnp
from jax import lax
from jax.experimental import pallas as pl
from jax.experimental.pallas import tpu as pltpu
from jax.sharding import Mesh, PartitionSpec as P

F32, BF16, I32 = jnp.float32, jnp.bfloat16, jnp.int32
LINE = ("zq", "zp")
DP = LINE + ("x", "c")
EXP = ("y", "zh")
NEAR = ("x", "c")
SHARE = ("zp", "x", "c")
RING = ("zh",) + LINE


def exchange(blocks, axes):
    return lax.all_to_all(blocks, axes, split_axis=0, concat_axis=0, tiled=True)


def dot(a, b, dims, out=BF16):
    return lax.dot_general(a, b, (dims, ((), ())), preferred_element_type=F32).astype(out)


def pack_kernel(capacity, slots, strip, xs, cs, hid_width, arrived, blocks):
    tall, width = arrived.shape
    rows = blocks.shape[1]
    quarter = hid_width // xs
    half = (width - hid_width) // cs
    full = lax.broadcasted_iota(I32, (rows, tall), 0)
    wanted = full // capacity * slots + full % capacity
    compact = (wanted == lax.broadcasted_iota(I32, (rows, tall), 1)).astype(BF16)
    kept = dot(compact, arrived[...], ((1,), (0,)))
    group = cs * strip
    place = lax.broadcasted_iota(I32, (hid_width, hid_width), 0)
    target = place // group % xs * quarter + place // (group * xs) * group + place % group
    sorter = (target == lax.broadcasted_iota(I32, (hid_width, hid_width), 1)).astype(BF16)
    hid = dot(kept[:, width - hid_width :], sorter, ((1,), (0,)))
    for x in range(xs):
        for c in range(cs):
            blocks[x * cs + c, :, :quarter] = hid[:, x * quarter : (x + 1) * quarter]
            blocks[x * cs + c, :, quarter:] = kept[:, c * half : (c + 1) * half]


def place_kernel(slots, ids, gates, hidden, out_grad, outgoing, ranks):
    tall = outgoing.shape[0]
    tok_rows, out_width = out_grad.shape
    square = (tok_rows, tok_rows)
    down, across = lax.broadcasted_iota(I32, square, 0), lax.broadcasted_iota(I32, square, 1)
    experts = lax.broadcasted_iota(I32, (tall // slots, tok_rows), 0)
    named = (experts == ids[...]).astype(F32)
    before = dot(named.astype(BF16), (down < across).astype(BF16), ((1,), (0,)), F32)
    rank = jnp.sum(named * before, axis=0, keepdims=True).astype(I32)
    ranks[...] = rank
    gate = jnp.sum(jnp.where(down == across, gates[...], 0.0), axis=1, keepdims=True)
    grads = (gate * out_grad[...].astype(F32)).astype(BF16)
    place = lax.broadcasted_iota(I32, (tall, tok_rows), 0)
    placer = (place == ids[...] * slots + rank).astype(BF16)
    outgoing[:, :out_width] = dot(placer, grads, ((1,), (0,)))
    outgoing[:, out_width:] = dot(placer, hidden[...], ((1,), (0,)))


def partial_kernel(capacity, halves, quarter, rows, partial):
    tall = rows.shape[0]
    expert = lax.broadcasted_iota(I32, (tall, quarter), 0) // capacity % halves
    hid, grads = rows[:, :quarter].astype(F32), rows[:, quarter:]
    for h in range(halves):
        kept = jnp.where(expert == h, hid, 0.0).astype(BF16)
        partial[h * quarter : (h + 1) * quarter, :] = dot(kept, grads, ((0,), (0,)), F32)


def shards(hidden, expert_ids, gate_weights, down_weight, out_grad):
    tok_rows, hid_width = hidden.shape
    out_width = out_grad.shape[1]
    columns, halves = lax.axis_size("y"), lax.axis_size("zh")
    experts = columns * halves
    xs, cs, near = (lax.axis_size(axes) for axes in ("x", "c", NEAR))
    capacity = 5 * tok_rows // (4 * experts)
    slots = capacity + -capacity % 4
    block = halves * slots
    tall = columns * block
    strip = hid_width // lax.axis_size(DP)
    half = lax.axis_index("zh")
    weight = down_weight[0]

    part = hid_width // lax.axis_size(SHARE)
    start = lax.axis_index(SHARE) * part
    share = lax.dynamic_slice_in_dim(weight, start, part, axis=0)
    share = lax.ppermute(share, "zh", [(0, 1), (1, 0)])

    expert_list = expert_ids[:, 0]
    outgoing, ranks = pl.pallas_call(
        functools.partial(place_kernel, slots),
        out_shape=(
            jax.ShapeDtypeStruct((tall, out_width + hid_width), BF16),
            jax.ShapeDtypeStruct((1, tok_rows), I32),
        ),
        compiler_params=pltpu.CompilerParams(vmem_limit_bytes=24 * 2**20),
        cost_estimate=pl.CostEstimate(
            flops=2 * tall * tok_rows * (hid_width + out_width),
            bytes_accessed=3 * 2**20,
            transcendentals=0,
        ),
    )(expert_ids.reshape(1, -1), gate_weights.reshape(1, -1), hidden, out_grad)
    row_rank = ranks[0]
    arrived = exchange(outgoing.reshape(columns, block, -1), "y").reshape(tall, -1)
    arrived, share = lax.optimization_barrier((arrived, share))
    beside = lax.ppermute(share, "zp", [(0, 1), (1, 0)])

    rows = experts * capacity
    near_rows = exchange(
        pl.pallas_call(
            functools.partial(pack_kernel, capacity, slots, strip, xs, cs, hid_width),
            out_shape=jax.ShapeDtypeStruct(
                (near, rows, hid_width // xs + out_width // cs), BF16
            ),
            compiler_params=pltpu.CompilerParams(vmem_limit_bytes=40 * 2**20),
            cost_estimate=pl.CostEstimate(
                flops=2 * rows * (tall * (hid_width + out_width) + hid_width**2),
                bytes_accessed=8 * 2**20,
                transcendentals=0,
            ),
        )(arrived),
        NEAR,
    ).reshape(near * rows, -1)
    full = jnp.arange(columns * capacity, dtype=I32)
    origin, rank = full // capacity, full % capacity
    odd = (rank % 2 == 1)[:, None]
    back_block = 16 * (-(-(capacity + (capacity + 1) // 2) // 16))
    short = columns * back_block

    def products(which, matrix, arrived):
        wanted = origin * block + which * slots + rank
        chosen = (wanted[:, None] == jnp.arange(tall, dtype=I32)[None, :]).astype(BF16)
        picked = dot(chosen, arrived, ((1,), (0,)))
        proj = dot(picked[:, out_width:], matrix, ((1,), (0,)))
        back = dot(picked[:, :out_width], matrix, ((1,), (1,)))
        zero = jnp.zeros((), BF16)
        pairs = jnp.concatenate(
            [jnp.where(odd, zero, back), jnp.where(odd, back, zero)], axis=1
        )
        spots = origin * back_block
        spots = jnp.concatenate([spots + rank, spots + capacity + rank // 2])
        spread = (jnp.arange(short, dtype=I32)[:, None] == spots[None, :]).astype(BF16)
        return dot(spread, jnp.concatenate([proj, pairs], axis=0), ((1,), (0,)))

    own_leaving = products(half, weight, arrived)
    near_rows, share, beside, own_leaving = lax.optimization_barrier(
        (near_rows, share, beside, own_leaving)
    )
    even = lax.axis_index("zp") == 0
    pair = jnp.stack([jnp.where(even, share, beside), jnp.where(even, beside, share)])
    other_weight = lax.all_gather(pair, NEAR, axis=1, tiled=True).reshape(hid_width, -1)
    partial_grad = pl.pallas_call(
        functools.partial(partial_kernel, capacity, halves, hid_width // xs),
        out_shape=jax.ShapeDtypeStruct((halves * hid_width // xs, out_width // cs), F32),
        compiler_params=pltpu.CompilerParams(vmem_limit_bytes=40 * 2**20),
        cost_estimate=pl.CostEstimate(
            flops=2 * near * rows * halves * (hid_width // xs) * (out_width // cs),
            bytes_accessed=6 * 2**20,
            transcendentals=0,
        ),
    )(near_rows)
    ring_sum = lax.psum_scatter(partial_grad, RING, scatter_dimension=0, tiled=True)

    own_leaving, _ = lax.optimization_barrier((own_leaving, partial_grad))
    own_back = exchange(own_leaving.reshape(columns, back_block, -1), "y").reshape(short, -1)
    arrived, own_back = lax.optimization_barrier((arrived, own_back))
    other_leaving = products(1 - half, other_weight, arrived)
    other_back = exchange(other_leaving.reshape(columns, back_block, -1), "y")
    other_back, ring_sum = lax.optimization_barrier((other_back.reshape(short, -1), ring_sum))
    returned = jnp.concatenate([own_back, other_back], axis=0)
    seat = jnp.where(expert_list % halves == half, 0, short) + expert_list // halves * back_block
    seats = jnp.concatenate([seat + row_rank, seat + capacity + row_rank // 2])
    fetcher = (jnp.arange(2 * short, dtype=I32)[:, None] == seats[None, :]).astype(BF16)
    fetched = dot(fetcher, returned, ((0,), (0,)), F32)
    projected = fetched[:tok_rows]
    hidden_grad = jnp.where(
        (row_rank % 2 == 1)[:, None],
        fetched[tok_rows:, hid_width:],
        fetched[tok_rows:, :hid_width],
    ).astype(BF16)
    layer_out = (gate_weights * projected).astype(BF16)
    gate_grad = jnp.sum(out_grad.astype(F32) * projected, axis=1, keepdims=True)

    core = lax.axis_index("c")
    first = core == 0
    kept = lax.dynamic_slice_in_dim(ring_sum, core * strip, strip, axis=0)
    given = lax.dynamic_slice_in_dim(ring_sum, (1 - core) * strip, strip, axis=0)
    taken = lax.ppermute(given, "c", [(0, 1), (1, 0)])
    weight_grad = jnp.concatenate(
        [jnp.where(first, kept, taken), jnp.where(first, taken, kept)], axis=1
    )
    return (layer_out, hidden_grad, gate_grad, weight_grad[None])


def solution(mesh):
    fine = Mesh(mesh.devices.reshape(4, 2, 4, 2, 8, 2), DP + EXP)
    tokens = P(DP + EXP, None)
    return jax.shard_map(
        shards,
        mesh=fine,
        in_specs=(tokens, tokens, tokens, P(EXP, None, None), tokens),
        out_specs=(tokens, tokens, tokens, P(EXP, DP, None)),
        check_vma=False,
    )
```

```python
import functools

import jax
import jax.numpy as jnp
from jax import lax
from jax.experimental import pallas as pl
from jax.experimental.pallas import tpu as pltpu
from jax.sharding import Mesh, PartitionSpec as P

F32, BF16, I32 = jnp.float32, jnp.bfloat16, jnp.int32
LINE = ("zq", "zp")
DP = LINE + ("x", "c")
EXP = ("y", "zh")
NEAR = ("x", "c")
SHARE = ("zp", "x", "c")
RING = ("zh",) + LINE


def exchange(blocks, axes):
    return lax.all_to_all(blocks, axes, split_axis=0, concat_axis=0, tiled=True)


def dot(a, b, dims, out=BF16):
    return lax.dot_general(a, b, (dims, ((), ())), preferred_element_type=F32).astype(out)


def pack_kernel(capacity, slots, strip, xs, cs, hid_width, arrived, blocks):
    tall, width = arrived.shape
    rows = blocks.shape[1]
    half = hid_width // cs
    quarter = (width - hid_width) // xs
    full = lax.broadcasted_iota(I32, (rows, tall), 0)
    wanted = full // capacity * slots + full % capacity
    compact = (wanted == lax.broadcasted_iota(I32, (rows, tall), 1)).astype(BF16)
    kept = dot(compact, arrived[...], ((1,), (0,)))
    group = cs * strip
    place = lax.broadcasted_iota(I32, (hid_width, hid_width), 0)
    row = place // (group * xs) * (xs * strip) + place // group % xs * strip + place % strip
    target = place // strip % cs * half + row
    sorter = (target == lax.broadcasted_iota(I32, (hid_width, hid_width), 1)).astype(BF16)
    hid = dot(kept[:, width - hid_width :], sorter, ((1,), (0,)))
    for x in range(xs):
        for c in range(cs):
            blocks[x * cs + c, :, :half] = hid[:, c * half : (c + 1) * half]
            blocks[x * cs + c, :, half:] = kept[:, x * quarter : (x + 1) * quarter]


def place_kernel(slots, ids, gates, hidden, out_grad, outgoing, ranks):
    tall = outgoing.shape[0]
    tok_rows, out_width = out_grad.shape
    square = (tok_rows, tok_rows)
    down, across = lax.broadcasted_iota(I32, square, 0), lax.broadcasted_iota(I32, square, 1)
    experts = lax.broadcasted_iota(I32, (tall // slots, tok_rows), 0)
    named = (experts == ids[...]).astype(F32)
    before = dot(named.astype(BF16), (down < across).astype(BF16), ((1,), (0,)), F32)
    rank = jnp.sum(named * before, axis=0, keepdims=True).astype(I32)
    ranks[...] = rank
    gate = jnp.sum(jnp.where(down == across, gates[...], 0.0), axis=1, keepdims=True)
    grads = (gate * out_grad[...].astype(F32)).astype(BF16)
    place = lax.broadcasted_iota(I32, (tall, tok_rows), 0)
    placer = (place == ids[...] * slots + rank).astype(BF16)
    outgoing[:, :out_width] = dot(placer, grads, ((1,), (0,)))
    outgoing[:, out_width:] = dot(placer, hidden[...], ((1,), (0,)))


def partial_kernel(capacity, halves, quarter, rows, partial):
    tall = rows.shape[0]
    expert = lax.broadcasted_iota(I32, (tall, quarter), 0) // capacity % halves
    hid, grads = rows[:, :quarter].astype(F32), rows[:, quarter:]
    for h in range(halves):
        kept = jnp.where(expert == h, hid, 0.0).astype(BF16)
        partial[h * quarter : (h + 1) * quarter, :] = dot(kept, grads, ((0,), (0,)), F32)


def shards(hidden, expert_ids, gate_weights, down_weight, out_grad):
    tok_rows, hid_width = hidden.shape
    out_width = out_grad.shape[1]
    columns, halves = lax.axis_size("y"), lax.axis_size("zh")
    experts = columns * halves
    xs, cs, near = (lax.axis_size(axes) for axes in ("x", "c", NEAR))
    capacity = 5 * tok_rows // (4 * experts)
    slots = capacity + -capacity % 4
    block = halves * slots
    tall = columns * block
    strip = hid_width // lax.axis_size(DP)
    half = lax.axis_index("zh")
    weight = down_weight[0]

    part = hid_width // lax.axis_size(SHARE)
    start = lax.axis_index(SHARE) * part
    share = lax.dynamic_slice_in_dim(weight, start, part, axis=0)
    share = lax.ppermute(share, "zh", [(0, 1), (1, 0)])

    expert_list = expert_ids[:, 0]
    outgoing, ranks = pl.pallas_call(
        functools.partial(place_kernel, slots),
        out_shape=(
            jax.ShapeDtypeStruct((tall, out_width + hid_width), BF16),
            jax.ShapeDtypeStruct((1, tok_rows), I32),
        ),
        compiler_params=pltpu.CompilerParams(vmem_limit_bytes=24 * 2**20),
        cost_estimate=pl.CostEstimate(
            flops=2 * tall * tok_rows * (hid_width + out_width),
            bytes_accessed=3 * 2**20,
            transcendentals=0,
        ),
    )(expert_ids.reshape(1, -1), gate_weights.reshape(1, -1), hidden, out_grad)
    row_rank = ranks[0]
    arrived = exchange(outgoing.reshape(columns, block, -1), "y").reshape(tall, -1)
    arrived, share = lax.optimization_barrier((arrived, share))
    beside = lax.ppermute(share, "zp", [(0, 1), (1, 0)])

    rows = experts * capacity
    near_rows = exchange(
        pl.pallas_call(
            functools.partial(pack_kernel, capacity, slots, strip, xs, cs, hid_width),
            out_shape=jax.ShapeDtypeStruct(
                (near, rows, hid_width // cs + out_width // xs), BF16
            ),
            compiler_params=pltpu.CompilerParams(vmem_limit_bytes=40 * 2**20),
            cost_estimate=pl.CostEstimate(
                flops=2 * rows * (tall * (hid_width + out_width) + hid_width**2),
                bytes_accessed=8 * 2**20,
                transcendentals=0,
            ),
        )(arrived),
        NEAR,
    ).reshape(near * rows, -1)
    full = jnp.arange(columns * capacity, dtype=I32)
    origin, rank = full // capacity, full % capacity
    odd = (rank % 2 == 1)[:, None]
    back_block = 16 * (-(-(capacity + (capacity + 1) // 2) // 16))
    short = columns * back_block

    def products(which, matrix, arrived):
        wanted = origin * block + which * slots + rank
        chosen = (wanted[:, None] == jnp.arange(tall, dtype=I32)[None, :]).astype(BF16)
        picked = dot(chosen, arrived, ((1,), (0,)))
        proj = dot(picked[:, out_width:], matrix, ((1,), (0,)))
        back = dot(picked[:, :out_width], matrix, ((1,), (1,)))
        zero = jnp.zeros((), BF16)
        pairs = jnp.concatenate(
            [jnp.where(odd, zero, back), jnp.where(odd, back, zero)], axis=1
        )
        spots = origin * back_block
        spots = jnp.concatenate([spots + rank, spots + capacity + rank // 2])
        spread = (jnp.arange(short, dtype=I32)[:, None] == spots[None, :]).astype(BF16)
        return dot(spread, jnp.concatenate([proj, pairs], axis=0), ((1,), (0,)))

    own_leaving = products(half, weight, arrived)
    near_rows, share, beside, own_leaving = lax.optimization_barrier(
        (near_rows, share, beside, own_leaving)
    )
    even = lax.axis_index("zp") == 0
    pair = jnp.stack([jnp.where(even, share, beside), jnp.where(even, beside, share)])
    other_weight = lax.all_gather(pair, NEAR, axis=1, tiled=True).reshape(hid_width, -1)
    partial_grad = pl.pallas_call(
        functools.partial(partial_kernel, capacity, halves, hid_width // cs),
        out_shape=jax.ShapeDtypeStruct((halves * hid_width // cs, out_width // xs), F32),
        compiler_params=pltpu.CompilerParams(vmem_limit_bytes=40 * 2**20),
        cost_estimate=pl.CostEstimate(
            flops=2 * near * rows * halves * (hid_width // cs) * (out_width // xs),
            bytes_accessed=6 * 2**20,
            transcendentals=0,
        ),
    )(near_rows)
    ring_sum = lax.psum_scatter(partial_grad, RING, scatter_dimension=0, tiled=True)

    own_leaving, _ = lax.optimization_barrier((own_leaving, partial_grad))
    own_back = exchange(own_leaving.reshape(columns, back_block, -1), "y").reshape(short, -1)
    arrived, own_back = lax.optimization_barrier((arrived, own_back))
    other_leaving = products(1 - half, other_weight, arrived)
    other_back = exchange(other_leaving.reshape(columns, back_block, -1), "y")
    other_back, ring_sum = lax.optimization_barrier((other_back.reshape(short, -1), ring_sum))
    returned = jnp.concatenate([own_back, other_back], axis=0)
    seat = jnp.where(expert_list % halves == half, 0, short) + expert_list // halves * back_block
    seats = jnp.concatenate([seat + row_rank, seat + capacity + row_rank // 2])
    fetcher = (jnp.arange(2 * short, dtype=I32)[:, None] == seats[None, :]).astype(BF16)
    fetched = dot(fetcher, returned, ((0,), (0,)), F32)
    projected = fetched[:tok_rows]
    hidden_grad = jnp.where(
        (row_rank % 2 == 1)[:, None],
        fetched[tok_rows:, hid_width:],
        fetched[tok_rows:, :hid_width],
    ).astype(BF16)
    layer_out = (gate_weights * projected).astype(BF16)
    gate_grad = jnp.sum(out_grad.astype(F32) * projected, axis=1, keepdims=True)

    mine = lax.axis_index("x")
    held = [
        lax.dynamic_slice_in_dim(ring_sum, (mine ^ k) * strip, strip, axis=0) for k in range(xs)
    ]
    held = [held[0]] + [
        lax.ppermute(held[k], "x", [(i, i ^ k) for i in range(xs)]) for k in range(1, xs)
    ]
    quarters = []
    for p in range(xs):
        chosen = held[0]
        for k in range(1, xs):
            chosen = jnp.where((mine ^ k) == p, held[k], chosen)
        quarters.append(chosen)
    weight_grad = jnp.concatenate(quarters, axis=1)
    return (layer_out, hidden_grad, gate_grad, weight_grad[None])


def solution(mesh):
    fine = Mesh(mesh.devices.reshape(4, 2, 4, 2, 8, 2), DP + EXP)
    tokens = P(DP + EXP, None)
    return jax.shard_map(
        shards,
        mesh=fine,
        in_specs=(tokens, tokens, tokens, P(EXP, None, None), tokens),
        out_specs=(tokens, tokens, tokens, P(EXP, DP, None)),
        check_vma=False,
    )
```
